32 devices in a mesh: batch: 2 (over x), gx: 4 (over y, core), gy: 4 (over z).
Axes of the slice: x: 2, y: 2, z: 4, core: 2. Of those that a mesh axis runs over, the one named last changes fastest.
Arguments:
- features: bfloat16 [128, 64, 4, 256], P(('batch', 'gx'), 'gy'), parts along dimension 0, may hold values from -6 to 6
- conv_weight: bfloat16 [6912, 256], replicated, may hold values from -0.078125 to 0.078125
- down_weight: bfloat16 [2048, 512], replicated, may hold values from -0.125 to 0.125
- norm_gain: float32 [512], replicated, may hold values from 0.1 to 1.9
- qkv_weight: bfloat16 [512, 1536], replicated, may hold values from -0.25 to 0.25
- out_weight: bfloat16 [512, 512], replicated, may hold values from -0.25 to 0.25
- upstream: bfloat16 [64, 32, 2, 512], P(('batch', 'gx'), 'gy'), parts along dimension 0, may hold values from -6 to 6
Outputs:
- grad_features: bfloat16 [128, 64, 4, 256], P(('batch', 'gx'), 'gy'), parts along dimension 0
- grad_conv: bfloat16 [13824, 256], P(('batch', 'gx', 'gy')), parts along dimension 0
- grad_down: bfloat16 [4096, 512], P(('batch', 'gx', 'gy')), parts along dimension 0
- grad_gain: float32 [1024], P(('batch', 'gx', 'gy')), parts along dimension 0
- grad_qkv: bfloat16 [1024, 1536], P(('batch', 'gx', 'gy')), parts along dimension 0
- grad_out: bfloat16 [1024, 512], P(('batch', 'gx', 'gy')), parts along dimension 0
The draws below stay inside these ranges and needn't reach their ends.
There are 2 independent parts, one for each index of `batch`. The reference program is written for one: setup_inputs(seed, part) draws one part's arguments, and reference() takes and returns one part's arrays. A program takes and returns all parts, laid end to end along the dimension named above; an argument that names none is the same for every part. Nothing has to cross between parts.
All inputs are finite; a program needn't handle non-finite values.
Results may differ from the reference program's by a relative error of at most 0.02.
Values may be sent and summed in bfloat16 or wider, within the bound.
A program may use at most 128 MiB of HBM per device.

```python
import jax
import jax.numpy as jnp
from jax import lax

C = 256
D = 512
H = 8
HD = 64
CX = 16
CY = 16
NZ = 4
NX = 64
NY = 64
TOKENS = 2048
N_GX = 4
N_GY = 4


def steps_of(stream_key, shape, split, smallest, top_value):
    def one(dim, parts):
        steps = jax.random.uniform(jax.random.fold_in(jax.random.fold_in(stream_key, 6), dim), (parts,), jnp.float32, smallest / len(split), top_value / len(split))
        return jnp.repeat(jnp.exp(steps), shape[dim] // parts).reshape((-1,) + (1,) * (len(shape) - dim - 1))

    level = one(*split[0])
    for cut in split[1:]:
        level = level * one(*cut)
    return level


def noise(rng, dims, scale, reach, pieces=(), kind=jnp.bfloat16):
    loudness = steps_of(rng, dims, pieces, -0.22, 0.18) if pieces else 1.0
    entries = jax.random.normal(rng, dims, jnp.float32) * scale * loudness
    return jnp.minimum(jnp.maximum(entries, -reach), reach).astype(kind)


def setup_inputs(seed: int = 0, part: int = 0) -> dict:
    arg_keys = jax.random.split(jax.random.key(seed), 8)
    part_splits = jax.random.split(jax.random.fold_in(arg_keys[7], part), 8)
    features = noise(part_splits[0], (NX, NY, NZ, C), 1.0, 6.0, ((0, 4), (1, 4)))
    conv_weight = noise(arg_keys[1], (27 * C, C), (27 * C) ** -0.5, 0.078125)
    down_weight = noise(arg_keys[2], (8 * C, D), (8 * C) ** -0.5, 0.125)
    norm_gain = jnp.clip(1.0 + 0.18 * jax.random.normal(arg_keys[3], (D,), jnp.float32), 0.1, 1.9)
    qkv_weight = noise(arg_keys[4], (D, 3 * D), D ** -0.5, 0.25)
    out_weight = noise(arg_keys[5], (D, D), D ** -0.5, 0.25)
    upstream = noise(part_splits[6], (NX // 2, NY // 2, NZ // 2, D), 1.0, 6.0, ((0, 4), (1, 4)))
    return dict(features=features, conv_weight=conv_weight, down_weight=down_weight, norm_gain=norm_gain, qkv_weight=qkv_weight, out_weight=out_weight, upstream=upstream)


precise = lax.Precision.HIGHEST

def rounded(value):
    return lax.optimization_barrier(value.astype(jnp.bfloat16)).astype(jnp.float32)

def to_tokens(volume):
    extent_x, extent_y, extent_z, channels = volume.shape
    grid = volume.reshape(extent_x // 2, 2, extent_y // 2, 2, extent_z // 2, 2, channels)
    grid = grid.transpose(0, 2, 4, 1, 3, 5, 6)
    return grid.reshape(extent_x * extent_y * extent_z // 8, 8 * channels)

def from_tokens(matrix, extent_x, extent_y, extent_z):
    channels = matrix.shape[1] // 8
    grid = matrix.reshape(extent_x // 2, extent_y // 2, extent_z // 2, 2, 2, 2, channels)
    grid = grid.transpose(0, 3, 1, 4, 2, 5, 6)
    return grid.reshape(extent_x, extent_y, extent_z, channels)

def by_tiles(rows, extent_x, extent_y, extent_z):
    width = rows.shape[1]
    grid = rows.reshape(N_GX, extent_x, N_GY, extent_y, extent_z, width)
    grid = grid.transpose(0, 2, 1, 3, 4, 5)
    return grid.reshape(N_GX * N_GY, extent_x * extent_y * extent_z, width)

def tile_sum(left, right, extent_x, extent_y, extent_z):
    left_tiles = by_tiles(left, extent_x, extent_y, extent_z)
    right_tiles = by_tiles(right, extent_x, extent_y, extent_z)
    partials = jnp.einsum('tra,trb->tab', left_tiles, right_tiles, precision=precise)
    return lax.optimization_barrier(jnp.sum(rounded(partials), axis=0))

def reference(features, conv_weight, down_weight, norm_gain, qkv_weight, out_weight, upstream):
    voxels = NX * NY * NZ
    score_scale = HD ** (-0.5)
    padded = jnp.pad(features.astype(jnp.float32), ((1, 1), (1, 1), (1, 1), (0, 0)))
    weights = conv_weight.astype(jnp.float32).reshape(27, C, C)
    offsets = [(ox, oy, oz) for ox in range(3) for oy in range(3) for oz in range(3)]
    hidden = jnp.zeros((voxels, C), jnp.float32)
    for position, (ox, oy, oz) in enumerate(offsets):
        window = padded[ox:ox + NX, oy:oy + NY, oz:oz + NZ].reshape(voxels, C)
        hidden = hidden + jnp.dot(window, weights[position], precision=precise)
    gate_sig = jax.nn.sigmoid(hidden)
    activation = rounded(hidden * gate_sig)
    tokens_in = to_tokens(activation.reshape(NX, NY, NZ, C))
    trunk_rows = jnp.dot(tokens_in, down_weight.astype(jnp.float32), precision=precise)
    mean_rows = lax.optimization_barrier(jnp.mean(trunk_rows, axis=-1, keepdims=True))
    centred = trunk_rows - mean_rows
    inverse_std = lax.rsqrt(lax.optimization_barrier(jnp.mean(centred * centred, axis=-1, keepdims=True)) + 1e-05)
    normed = centred * inverse_std
    normed_b = rounded(normed * norm_gain)
    qkv_rows = rounded(jnp.dot(normed_b, qkv_weight.astype(jnp.float32), precision=precise))
    queries = qkv_rows[:, :D].reshape(TOKENS, H, HD)
    keys_h = qkv_rows[:, D:2 * D].reshape(TOKENS, H, HD)
    values_h = qkv_rows[:, 2 * D:].reshape(TOKENS, H, HD)
    scores = jnp.einsum('ihe,jhe->hij', queries, keys_h, precision=precise) * score_scale
    exp_scores = jnp.exp(scores)
    totals = lax.optimization_barrier(jnp.sum(exp_scores, axis=-1, keepdims=True))
    attn_probs = exp_scores / totals
    probs_b = rounded(attn_probs)
    attended = rounded(jnp.einsum('hij,jhe->ihe', probs_b, values_h, precision=precise).reshape(TOKENS, D))
    cotangent = upstream.reshape(TOKENS, D).astype(jnp.float32)
    tok_x = CX // 2
    tok_y = CY // 2
    tok_z = NZ // 2
    grad_out = tile_sum(attended, cotangent, tok_x, tok_y, tok_z).astype(jnp.bfloat16)
    d_attended = rounded(jnp.dot(cotangent, out_weight.astype(jnp.float32).T, precision=precise))
    d_att_h = d_attended.reshape(TOKENS, H, HD)
    d_probs = rounded(jnp.einsum('ihe,jhe->hij', d_att_h, values_h, precision=precise))
    row_delta = lax.optimization_barrier(jnp.sum(attn_probs * d_probs, axis=-1, keepdims=True))
    d_scores = attn_probs * (d_probs - row_delta)
    d_queries = jnp.einsum('hij,jhe->ihe', d_scores, keys_h, precision=precise) * score_scale
    d_keys = jnp.einsum('hij,ihe->jhe', d_scores, queries, precision=precise) * score_scale
    d_values = jnp.einsum('hij,ihe->jhe', probs_b, d_att_h, precision=precise)
    d_qkv = rounded(jnp.concatenate([d_queries.reshape(TOKENS, D), d_keys.reshape(TOKENS, D), d_values.reshape(TOKENS, D)], axis=1))
    grad_qkv = tile_sum(normed_b, d_qkv, tok_x, tok_y, tok_z).astype(jnp.bfloat16)
    d_normed = rounded(jnp.dot(d_qkv, qkv_weight.astype(jnp.float32).T, precision=precise))
    d_hat = d_normed * norm_gain
    grad_gain = lax.optimization_barrier(jnp.sum(d_normed * normed, axis=0))
    d_trunk = cotangent + inverse_std * (d_hat - lax.optimization_barrier(jnp.mean(d_hat, axis=-1, keepdims=True)) - normed * lax.optimization_barrier(jnp.mean(d_hat * normed, axis=-1, keepdims=True)))
    grad_down = tile_sum(tokens_in, d_trunk, tok_x, tok_y, tok_z).astype(jnp.bfloat16)
    d_activation = rounded(jnp.dot(d_trunk, down_weight.astype(jnp.float32).T, precision=precise))
    d_act_grid = from_tokens(d_activation, NX, NY, NZ).reshape(voxels, C)
    d_hidden = rounded(d_act_grid * gate_sig * (1.0 + hidden * (1.0 - gate_sig)))
    d_padded = jnp.pad(d_hidden.reshape(NX, NY, NZ, C), ((1, 1), (1, 1), (1, 1), (0, 0)))
    grad_rows = []
    grad_features = jnp.zeros((voxels, C), jnp.float32)
    for position, (ox, oy, oz) in enumerate(offsets):
        window = padded[ox:ox + NX, oy:oy + NY, oz:oz + NZ].reshape(voxels, C)
        grad_rows.append(tile_sum(window, d_hidden, CX, CY, NZ))
        flipped = d_padded[2 - ox:2 - ox + NX, 2 - oy:2 - oy + NY, 2 - oz:2 - oz + NZ].reshape(voxels, C)
        grad_features = grad_features + jnp.dot(flipped, weights[position].T, precision=precise)
    grad_conv = jnp.concatenate(grad_rows, axis=0).astype(jnp.bfloat16)
    return (grad_features.reshape(NX, NY, NZ, C).astype(jnp.bfloat16), grad_conv, grad_down, grad_gain, grad_qkv, grad_out)
```

```python
import functools

import jax
import jax.numpy as jnp
from jax import lax
from jax.experimental import pallas as pl
from jax.experimental.pallas import tpu as pltpu
from jax.sharding import PartitionSpec as P

H = 8
HD = 64
MESH = pl.DeviceIdType.MESH
BF = jnp.bfloat16
F32 = jnp.float32


def halo(block, sides):
    for axis, dim in sides:
        count = lax.axis_size(axis)
        forward = [(i, i + 1) for i in range(count - 1)]
        backward = [(target, source) for source, target in forward]
        low = lax.ppermute(
            lax.slice_in_dim(block, block.shape[dim] - 1, None, axis=dim), axis, forward
        )
        high = lax.ppermute(lax.slice_in_dim(block, 0, 1, axis=dim), axis, backward)
        block = jnp.concatenate([low, block, high], axis=dim)
    return block


def patches_of(padded, z, x, y, flipped):
    shifted = [padded[:, :, o : o + y] for o in range(3)]
    pieces = []
    for ox in range(3):
        for oy in range(3):
            for oz in range(3):
                sx, sy, sz = (2 - ox, 2 - oy, 2 - oz) if flipped else (ox, oy, oz)
                pieces.append(shifted[sy][sz : sz + z, sx : sx + x])
    joined = jnp.concatenate(pieces, axis=3)
    return joined.reshape(z * x * y, joined.shape[3])


def to_tokens(cells, z, x, y):
    channels = cells.shape[-1]
    grid = cells.reshape(z // 2, 2, x // 2, 2, y // 2, 2, channels)
    grid = grid.transpose(2, 4, 0, 3, 5, 1, 6)
    return grid.reshape(z * x * y // 8, 8 * channels)


def from_tokens(matrix, z, x, y):
    channels = matrix.shape[1] // 8
    grid = matrix.reshape(x // 2, y // 2, z // 2, 2, 2, 2, channels)
    grid = grid.transpose(2, 5, 0, 3, 1, 4, 6)
    return grid.reshape(z * x * y, channels)


def peer_of(index, n_gy):
    return {"gx": index // n_gy, "gy": lax.rem(index, n_gy)}


def attention_kernel(
    n, n_gy, send_ref, dqo_ref, dkv_ref, recv, back, home, e_buf, dp_buf, acc, s1, r1, s2, r2
):
    rows = send_ref.shape[1]
    half = rows // 3
    me = lax.axis_index("gx") * n_gy + lax.axis_index("gy")
    barrier = pltpu.get_barrier_semaphore()

    def greet(i, carry):
        pl.semaphore_signal(
            barrier, inc=1, device_id=peer_of(lax.rem(me + i, n), n_gy), device_id_type=MESH
        )
        return carry

    lax.fori_loop(1, n, greet, 0)
    pl.semaphore_wait(barrier, n - 1)

    def send(src, dst, ssem, rsem):
        def body(i, carry):
            peer = lax.rem(me + i, n)
            pltpu.make_async_remote_copy(
                src_ref=src.at[peer],
                dst_ref=dst.at[me],
                send_sem=ssem.at[i],
                recv_sem=rsem.at[i],
                device_id=peer_of(peer, n_gy),
                device_id_type=MESH,
            ).start()
            return carry

        lax.fori_loop(1, n, body, 0)

    def finish(src, dst, ssem, rsem):
        def body(i, carry):
            peer = lax.rem(me + i, n)
            source = lax.rem(me + n - i, n)
            pltpu.make_async_remote_copy(
                src_ref=src.at[peer],
                dst_ref=dst.at[source],
                send_sem=ssem.at[i],
                recv_sem=rsem.at[i],
                device_id=peer_of(peer, n_gy),
                device_id_type=MESH,
            ).wait()
            return carry

        lax.fori_loop(1, n, body, 0)

    send(send_ref, recv, s1, r1)
    recv[pl.ds(me, 1)] = send_ref[pl.ds(me, 1)]
    finish(send_ref, recv, s1, r1)

    group = 256 // half
    kgroup = 256 // (2 * half)
    n_k = n // kgroup
    low = lax.broadcasted_iota(jnp.int32, (256, 128), 1) < HD
    acc[...] = jnp.zeros_like(acc)

    def keys_of(kc):
        return recv[kc * kgroup : (kc + 1) * kgroup, half:].reshape(256, 128)

    def block(b, carry):
        qd = recv[pl.ds(b * group, group), :half].reshape(256, 128)
        zero = jnp.zeros_like(qd)
        q0 = jnp.where(low, qd * BF(HD**-0.5), zero)
        d0 = jnp.where(low, zero, qd)
        nt = (((1,), (1,)), ((), ()))
        total = jnp.zeros((1, 256), F32)
        delta = jnp.zeros((1, 256), F32)
        for kc in range(n_k):
            kv = keys_of(kc)
            e = jnp.exp(lax.dot_general(kv, q0, nt, preferred_element_type=F32))
            dp = lax.dot_general(kv, d0, nt, preferred_element_type=F32)
            e_buf[kc] = e
            dp_buf[kc] = dp
            total = total + jnp.sum(e, axis=0, keepdims=True)
            delta = delta + jnp.sum(e * dp, axis=0, keepdims=True)
        inverse = 1.0 / total
        delta = delta * inverse
        qd0 = jnp.concatenate([q0, d0], axis=0)
        dq_t = jnp.zeros((128, 256), F32)
        o_t = jnp.zeros((128, 256), F32)
        for kc in range(n_k):
            p = e_buf[kc] * inverse
            ds = (p * (dp_buf[kc] - delta)).astype(BF)
            pb = p.astype(BF)
            kv_t = keys_of(kc).T
            dq_t = dq_t + jnp.dot(kv_t, ds, preferred_element_type=F32)
            o_t = o_t + jnp.dot(kv_t, pb, preferred_element_type=F32)
            acc[kc] += jnp.dot(
                jnp.concatenate([ds, pb], axis=1), qd0, preferred_element_type=F32
            )
        dqo_t = jnp.concatenate([dq_t[:HD] * HD**-0.5, o_t[HD:]], axis=0)
        back[pl.ds(b * group, group), :half] = dqo_t.T.astype(BF).reshape(group, half, 128)
        return carry

    lax.fori_loop(0, n // group, block, 0)
    for kc in range(n_k):
        back[kc * kgroup : (kc + 1) * kgroup, half:] = (
            acc[kc].astype(BF).reshape(kgroup, 2 * half, 128)
        )

    send(back, home, s2, r2)
    home[pl.ds(me, 1)] = back[pl.ds(me, 1)]
    finish(back, home, s2, r2)
    for h in range(H):
        dqo_ref[h] = home[2 * h : 2 * h + 2, :half].reshape(2 * half, 128)
        dkv_ref[h] = (home[2 * h, half:].astype(F32) + home[2 * h + 1, half:].astype(F32)).astype(
            BF
        )


def attention(send):
    n_gy = lax.axis_size("gy")
    n, rows, width = send.shape
    tokens = rows // 3 * 2
    vm = pl.BlockSpec(memory_space=pltpu.VMEM)
    n_k = n * tokens // 256
    return pl.pallas_call(
        functools.partial(attention_kernel, n, n_gy),
        out_shape=(
            jax.ShapeDtypeStruct((H, tokens, width), BF),
            jax.ShapeDtypeStruct((H, tokens, width), BF),
        ),
        in_specs=[vm],
        out_specs=(vm, vm),
        scratch_shapes=[
            pltpu.VMEM(send.shape, BF),
            pltpu.VMEM(send.shape, BF),
            pltpu.VMEM(send.shape, BF),
            pltpu.VMEM((n_k, 256, 256), F32),
            pltpu.VMEM((n_k, 256, 256), F32),
            pltpu.VMEM((n_k, 256, 128), F32),
            pltpu.SemaphoreType.DMA((n,)),
            pltpu.SemaphoreType.DMA((n,)),
            pltpu.SemaphoreType.DMA((n,)),
            pltpu.SemaphoreType.DMA((n,)),
        ],
        compiler_params=pltpu.CompilerParams(
            collective_id=0, has_side_effects=True, vmem_limit_bytes=40 * 1024 * 1024
        ),
        cost_estimate=pl.CostEstimate(
            flops=2_000_000_000, bytes_accessed=2_000_000, transcendentals=2_000_000
        ),
    )(send)


def local(features, conv_weight, down_weight, norm_gain, qkv_weight, out_weight, upstream):
    x, y, z, channels = features.shape
    width = out_weight.shape[0]
    group = lax.axis_size("gx") * lax.axis_size("gy")
    cells = features.transpose(2, 0, 1, 3)
    padded = halo(cells, (("gx", 1), ("gy", 2)))
    padded = jnp.pad(padded, ((1, 1), (0, 0), (0, 0), (0, 0)))
    patches = patches_of(padded, z, x, y, False)
    hidden = jnp.dot(patches, conv_weight, preferred_element_type=F32)
    gate_sig = jax.nn.sigmoid(hidden)
    activation = (hidden * gate_sig).astype(BF)
    tokens_in = to_tokens(activation, z, x, y)
    tokens = tokens_in.shape[0]
    trunk = jnp.dot(tokens_in, down_weight, preferred_element_type=F32)
    centred = trunk - jnp.mean(trunk, axis=-1, keepdims=True)
    inverse_std = lax.rsqrt(jnp.mean(centred * centred, axis=-1, keepdims=True) + 1e-05)
    normed = centred * inverse_std
    normed_b = (normed * norm_gain).astype(BF)
    cotangent = upstream.reshape(tokens, width)

    w_kv = (
        qkv_weight[:, width:].reshape(width, 2, H, HD).transpose(0, 2, 1, 3).reshape(width, -1)
    )
    w_q = qkv_weight[:, :width]
    kv = jnp.dot(normed_b, w_kv, preferred_element_type=F32).astype(BF)
    queries = jnp.dot(normed_b, w_q, preferred_element_type=F32).astype(BF)
    d_attended = lax.dot_general(
        cotangent, out_weight, (((1,), (1,)), ((), ())), preferred_element_type=F32
    ).astype(BF)
    qd = jnp.concatenate(
        [queries.reshape(tokens, H, HD), d_attended.reshape(tokens, H, HD)], axis=2
    )
    qd = qd.reshape(2, tokens // 2, H, 2 * HD).transpose(2, 0, 1, 3)
    kv_h = kv.reshape(tokens, H, 2 * HD).transpose(1, 0, 2)
    kv_h = jnp.broadcast_to(kv_h[:, None], (H, 2, tokens, 2 * HD))
    send = jnp.concatenate([qd, kv_h], axis=2).reshape(group, tokens * 3 // 2, 2 * HD)
    dqo, dkv = attention(send)
    dqo = dqo.transpose(1, 0, 2)
    attended = dqo[:, :, HD:].reshape(tokens, width)
    d_q = dqo[:, :, :HD].reshape(tokens, width)
    d_kv = dkv.transpose(1, 0, 2).reshape(tokens, 2 * width)
    d_qkv = jnp.concatenate([d_q, d_kv], axis=1)
    w_all = jnp.concatenate([w_q, w_kv], axis=1)

    tn = (((0,), (0,)), ((), ()))
    nt = (((1,), (1,)), ((), ()))
    out_part = lax.dot_general(attended, cotangent, tn, preferred_element_type=F32)
    qkv_part = lax.dot_general(normed_b, d_qkv, tn, preferred_element_type=F32)
    d_normed = lax.dot_general(d_qkv, w_all, nt, preferred_element_type=F32)
    d_hat = d_normed * norm_gain
    gain_part = jnp.sum(d_normed * normed, axis=0)
    d_trunk = cotangent.astype(F32) + inverse_std * (
        d_hat
        - jnp.mean(d_hat, axis=-1, keepdims=True)
        - normed * jnp.mean(d_hat * normed, axis=-1, keepdims=True)
    )
    d_trunk = d_trunk.astype(BF)
    down_part = lax.dot_general(tokens_in, d_trunk, tn, preferred_element_type=F32)
    d_activation = lax.dot_general(d_trunk, down_weight, nt, preferred_element_type=F32).astype(BF)
    d_act = from_tokens(d_activation, z, x, y).astype(F32)
    d_hidden = (d_act * gate_sig * (1.0 + hidden * (1.0 - gate_sig))).astype(BF)
    conv_part = lax.dot_general(patches, d_hidden, tn, preferred_element_type=F32)
    d_padded = halo(d_hidden.reshape(z, x, y, channels), (("gx", 1), ("gy", 2)))
    d_padded = jnp.pad(d_padded, ((1, 1), (0, 0), (0, 0), (0, 0)))
    d_patches = patches_of(d_padded, z, x, y, True)
    conv_flip = (
        conv_weight.reshape(27, channels, channels)
        .transpose(0, 2, 1)
        .reshape(27 * channels, channels)
    )
    grad_features = jnp.dot(d_patches, conv_flip, preferred_element_type=F32).astype(BF)
    grad_features = grad_features.reshape(z, x, y, channels).transpose(1, 2, 0, 3)
    conv_sum, down_sum, qkv_sum, out_sum, gain_sum = reduce_all(
        conv_part.astype(BF), down_part.astype(BF), qkv_part.astype(BF), out_part.astype(BF),
        gain_part,
    )
    kv_sum = qkv_sum[:, width:].reshape(-1, H, 2, HD).transpose(0, 2, 1, 3).reshape(-1, 2 * width)
    qkv_sum = jnp.concatenate([qkv_sum[:, :width], kv_sum], axis=1)
    return grad_features, conv_sum, down_sum, gain_sum, qkv_sum, out_sum


def reduce_all(conv_part, down_part, qkv_part, out_part, gain_part):
    def scatter(part):
        return lax.psum_scatter(part, ("gx", "gy"), scatter_dimension=0, tiled=True)

    gains = lax.all_gather(gain_part, ("gx", "gy"), axis=0)
    me = lax.axis_index(("gx", "gy"))
    size = gain_part.shape[0] // gains.shape[0]
    gain_sum = lax.dynamic_slice_in_dim(jnp.sum(gains, axis=0), me * size, size, 0)
    return scatter(conv_part), scatter(down_part), scatter(qkv_part), scatter(out_part), gain_sum


def solution(mesh):
    placed = (
        P(("batch", "gx"), "gy", None, None),
        P(),
        P(),
        P(),
        P(),
        P(),
        P(("batch", "gx"), "gy", None, None),
    )
    return jax.shard_map(
        local,
        mesh=mesh,
        in_specs=placed,
        out_specs=(
            P(("batch", "gx"), "gy", None, None),
            P(("batch", "gx", "gy"), None),
            P(("batch", "gx", "gy"), None),
            P(("batch", "gx", "gy")),
            P(("batch", "gx", "gy"), None),
            P(("batch", "gx", "gy"), None),
        ),
        check_vma=False,
    )
```

```python
import functools

import jax
import jax.numpy as jnp
from jax import lax
from jax.experimental import pallas as pl
from jax.experimental.pallas import tpu as pltpu
from jax.sharding import PartitionSpec as P

H = 8
HD = 64
MESH = pl.DeviceIdType.MESH
BF = jnp.bfloat16
F32 = jnp.float32


def halo(block, sides):
    for axis, dim in sides:
        count = lax.axis_size(axis)
        forward = [(i, i + 1) for i in range(count - 1)]
        backward = [(target, source) for source, target in forward]
        low = lax.ppermute(
            lax.slice_in_dim(block, block.shape[dim] - 1, None, axis=dim), axis, forward
        )
        high = lax.ppermute(lax.slice_in_dim(block, 0, 1, axis=dim), axis, backward)
        block = jnp.concatenate([low, block, high], axis=dim)
    return block


def patches_of(padded, z, x, y, flipped):
    shifted = [padded[:, :, o : o + y] for o in range(3)]
    pieces = []
    for ox in range(3):
        for oy in range(3):
            for oz in range(3):
                sx, sy, sz = (2 - ox, 2 - oy, 2 - oz) if flipped else (ox, oy, oz)
                pieces.append(shifted[sy][sz : sz + z, sx : sx + x])
    joined = jnp.concatenate(pieces, axis=3)
    return joined.reshape(z * x * y, joined.shape[3])


def to_tokens(cells, z, x, y):
    channels = cells.shape[-1]
    grid = cells.reshape(z // 2, 2, x // 2, 2, y // 2, 2, channels)
    grid = grid.transpose(2, 4, 0, 3, 5, 1, 6)
    return grid.reshape(z * x * y // 8, 8 * channels)


def from_tokens(matrix, z, x, y):
    channels = matrix.shape[1] // 8
    grid = matrix.reshape(x // 2, y // 2, z // 2, 2, 2, 2, channels)
    grid = grid.transpose(2, 5, 0, 3, 1, 4, 6)
    return grid.reshape(z * x * y, channels)


def peer_of(index, n_gy):
    return {"gx": index // n_gy, "gy": lax.rem(index, n_gy)}


def attention_kernel(
    n, n_gy, send_ref, dqo_ref, dkv_ref, recv, back, home, e_buf, dp_buf, acc, s1, r1, s2, r2
):
    rows = send_ref.shape[1]
    half = rows // 3
    me = lax.axis_index("gx") * n_gy + lax.axis_index("gy")
    barrier = pltpu.get_barrier_semaphore()

    def greet(i, carry):
        pl.semaphore_signal(
            barrier, inc=1, device_id=peer_of(lax.rem(me + i, n), n_gy), device_id_type=MESH
        )
        return carry

    lax.fori_loop(1, n, greet, 0)
    pl.semaphore_wait(barrier, n - 1)

    def send(src, dst, ssem, rsem):
        def body(i, carry):
            peer = lax.rem(me + i, n)
            pltpu.make_async_remote_copy(
                src_ref=src.at[peer],
                dst_ref=dst.at[me],
                send_sem=ssem.at[i],
                recv_sem=rsem.at[i],
                device_id=peer_of(peer, n_gy),
                device_id_type=MESH,
            ).start()
            return carry

        lax.fori_loop(1, n, body, 0)

    def finish(src, dst, ssem, rsem):
        def body(i, carry):
            peer = lax.rem(me + i, n)
            source = lax.rem(me + n - i, n)
            pltpu.make_async_remote_copy(
                src_ref=src.at[peer],
                dst_ref=dst.at[source],
                send_sem=ssem.at[i],
                recv_sem=rsem.at[i],
                device_id=peer_of(peer, n_gy),
                device_id_type=MESH,
            ).wait()
            return carry

        lax.fori_loop(1, n, body, 0)

    send(send_ref, recv, s1, r1)
    recv[pl.ds(me, 1)] = send_ref[pl.ds(me, 1)]
    finish(send_ref, recv, s1, r1)

    group = 256 // half
    kgroup = 256 // (2 * half)
    n_k = n // kgroup
    low = lax.broadcasted_iota(jnp.int32, (256, 128), 1) < HD
    acc[...] = jnp.zeros_like(acc)

    def keys_of(kc):
        return recv[kc * kgroup : (kc + 1) * kgroup, half:].reshape(256, 128)

    def block(b, carry):
        qd = recv[pl.ds(b * group, group), :half].reshape(256, 128)
        zero = jnp.zeros_like(qd)
        q0 = jnp.where(low, qd * BF(HD**-0.5), zero)
        d0 = jnp.where(low, zero, qd)
        nt = (((1,), (1,)), ((), ()))
        total = jnp.zeros((1, 256), F32)
        delta = jnp.zeros((1, 256), F32)
        for kc in range(n_k):
            kv = keys_of(kc)
            e = jnp.exp(lax.dot_general(kv, q0, nt, preferred_element_type=F32))
            dp = lax.dot_general(kv, d0, nt, preferred_element_type=F32)
            e_buf[kc] = e
            dp_buf[kc] = dp
            total = total + jnp.sum(e, axis=0, keepdims=True)
            delta = delta + jnp.sum(e * dp, axis=0, keepdims=True)
        inverse = 1.0 / total
        delta = delta * inverse
        qd0 = jnp.concatenate([q0, d0], axis=0)
        dq_t = jnp.zeros((128, 256), F32)
        o_t = jnp.zeros((128, 256), F32)
        for kc in range(n_k):
            p = e_buf[kc] * inverse
            ds = (p * (dp_buf[kc] - delta)).astype(BF)
            pb = p.astype(BF)
            kv_t = keys_of(kc).T
            dq_t = dq_t + jnp.dot(kv_t, ds, preferred_element_type=F32)
            o_t = o_t + jnp.dot(kv_t, pb, preferred_element_type=F32)
            acc[kc] += jnp.dot(
                jnp.concatenate([ds, pb], axis=1), qd0, preferred_element_type=F32
            )
        dqo_t = jnp.concatenate([dq_t[:HD] * HD**-0.5, o_t[HD:]], axis=0)
        back[pl.ds(b * group, group), :half] = dqo_t.T.astype(BF).reshape(group, half, 128)
        return carry

    lax.fori_loop(0, n // group, block, 0)
    for kc in range(n_k):
        back[kc * kgroup : (kc + 1) * kgroup, half:] = (
            acc[kc].astype(BF).reshape(kgroup, 2 * half, 128)
        )

    send(back, home, s2, r2)
    home[pl.ds(me, 1)] = back[pl.ds(me, 1)]
    finish(back, home, s2, r2)
    for h in range(H):
        dqo_ref[h] = home[2 * h : 2 * h + 2, :half].reshape(2 * half, 128)
        dkv_ref[h] = (home[2 * h, half:].astype(F32) + home[2 * h + 1, half:].astype(F32)).astype(
            BF
        )


def attention(send):
    n_gy = lax.axis_size("gy")
    n, rows, width = send.shape
    tokens = rows // 3 * 2
    vm = pl.BlockSpec(memory_space=pltpu.VMEM)
    n_k = n * tokens // 256
    return pl.pallas_call(
        functools.partial(attention_kernel, n, n_gy),
        out_shape=(
            jax.ShapeDtypeStruct((H, tokens, width), BF),
            jax.ShapeDtypeStruct((H, tokens, width), BF),
        ),
        in_specs=[vm],
        out_specs=(vm, vm),
        scratch_shapes=[
            pltpu.VMEM(send.shape, BF),
            pltpu.VMEM(send.shape, BF),
            pltpu.VMEM(send.shape, BF),
            pltpu.VMEM((n_k, 256, 256), F32),
            pltpu.VMEM((n_k, 256, 256), F32),
            pltpu.VMEM((n_k, 256, 128), F32),
            pltpu.SemaphoreType.DMA((n,)),
            pltpu.SemaphoreType.DMA((n,)),
            pltpu.SemaphoreType.DMA((n,)),
            pltpu.SemaphoreType.DMA((n,)),
        ],
        compiler_params=pltpu.CompilerParams(
            collective_id=0, has_side_effects=True, vmem_limit_bytes=40 * 1024 * 1024
        ),
        cost_estimate=pl.CostEstimate(
            flops=2_000_000_000, bytes_accessed=2_000_000, transcendentals=2_000_000
        ),
    )(send)


def local(features, conv_weight, down_weight, norm_gain, qkv_weight, out_weight, upstream):
    x, y, z, channels = features.shape
    width = out_weight.shape[0]
    group = lax.axis_size("gx") * lax.axis_size("gy")
    cells = features.transpose(2, 0, 1, 3)
    padded = halo(cells, (("gx", 1), ("gy", 2)))
    padded = jnp.pad(padded, ((1, 1), (0, 0), (0, 0), (0, 0)))
    patches = patches_of(padded, z, x, y, False)
    hidden = jnp.dot(patches, conv_weight, preferred_element_type=F32)
    gate_sig = jax.nn.sigmoid(hidden)
    activation = (hidden * gate_sig).astype(BF)
    tokens_in = to_tokens(activation, z, x, y)
    tokens = tokens_in.shape[0]
    trunk = jnp.dot(tokens_in, down_weight, preferred_element_type=F32)
    centred = trunk - jnp.mean(trunk, axis=-1, keepdims=True)
    inverse_std = lax.rsqrt(jnp.mean(centred * centred, axis=-1, keepdims=True) + 1e-05)
    normed = centred * inverse_std
    normed_b = (normed * norm_gain).astype(BF)
    cotangent = upstream.reshape(tokens, width)

    w_kv = (
        qkv_weight[:, width:].reshape(width, 2, H, HD).transpose(0, 2, 1, 3).reshape(width, -1)
    )
    w_q = qkv_weight[:, :width]
    kv = jnp.dot(normed_b, w_kv, preferred_element_type=F32).astype(BF)
    queries = jnp.dot(normed_b, w_q, preferred_element_type=F32).astype(BF)
    d_attended = lax.dot_general(
        cotangent, out_weight, (((1,), (1,)), ((), ())), preferred_element_type=F32
    ).astype(BF)
    qd = jnp.concatenate(
        [queries.reshape(tokens, H, HD), d_attended.reshape(tokens, H, HD)], axis=2
    )
    qd = qd.reshape(2, tokens // 2, H, 2 * HD).transpose(2, 0, 1, 3)
    kv_h = kv.reshape(tokens, H, 2 * HD).transpose(1, 0, 2)
    kv_h = jnp.broadcast_to(kv_h[:, None], (H, 2, tokens, 2 * HD))
    send = jnp.concatenate([qd, kv_h], axis=2).reshape(group, tokens * 3 // 2, 2 * HD)
    dqo, dkv = attention(send)
    dqo = dqo.transpose(1, 0, 2)
    attended = dqo[:, :, HD:].reshape(tokens, width)
    d_q = dqo[:, :, :HD].reshape(tokens, width)
    d_kv = dkv.transpose(1, 0, 2).reshape(tokens, 2 * width)
    d_qkv = jnp.concatenate([d_q, d_kv], axis=1)
    w_all = jnp.concatenate([w_q, w_kv], axis=1)

    tn = (((0,), (0,)), ((), ()))
    nt = (((1,), (1,)), ((), ()))
    out_part = lax.dot_general(attended, cotangent, tn, preferred_element_type=F32)
    qkv_part = lax.dot_general(normed_b, d_qkv, tn, preferred_element_type=F32)
    d_normed = lax.dot_general(d_qkv, w_all, nt, preferred_element_type=F32)
    d_hat = d_normed * norm_gain
    gain_part = jnp.sum(d_normed * normed, axis=0)
    d_trunk = cotangent.astype(F32) + inverse_std * (
        d_hat
        - jnp.mean(d_hat, axis=-1, keepdims=True)
        - normed * jnp.mean(d_hat * normed, axis=-1, keepdims=True)
    )
    d_trunk = d_trunk.astype(BF)
    down_part = lax.dot_general(tokens_in, d_trunk, tn, preferred_element_type=F32)
    d_activation = lax.dot_general(d_trunk, down_weight, nt, preferred_element_type=F32).astype(BF)
    d_act = from_tokens(d_activation, z, x, y).astype(F32)
    d_hidden = (d_act * gate_sig * (1.0 + hidden * (1.0 - gate_sig))).astype(BF)
    conv_part = lax.dot_general(patches, d_hidden, tn, preferred_element_type=F32)
    d_padded = halo(d_hidden.reshape(z, x, y, channels), (("gx", 1), ("gy", 2)))
    d_padded = jnp.pad(d_padded, ((1, 1), (0, 0), (0, 0), (0, 0)))
    d_patches = patches_of(d_padded, z, x, y, True)
    conv_flip = (
        conv_weight.reshape(27, channels, channels)
        .transpose(0, 2, 1)
        .reshape(27 * channels, channels)
    )
    grad_features = jnp.dot(d_patches, conv_flip, preferred_element_type=F32).astype(BF)
    grad_features = grad_features.reshape(z, x, y, channels).transpose(1, 2, 0, 3)
    conv_sum, down_sum, qkv_sum, out_sum, gain_sum = reduce_all(
        conv_part.astype(BF), down_part.astype(BF), qkv_part.astype(BF), out_part.astype(BF),
        gain_part,
    )
    kv_sum = qkv_sum[:, width:].reshape(-1, H, 2, HD).transpose(0, 2, 1, 3).reshape(-1, 2 * width)
    qkv_sum = jnp.concatenate([qkv_sum[:, :width], kv_sum], axis=1)
    return grad_features, conv_sum, down_sum, gain_sum, qkv_sum, out_sum


CORE = ("gx", 1, 1)
Y = ("gx", 2, 0)
Z_NEAR = ("gy", 1, 3)
Z_FAR = ("gy", 2, 2)


def swap(array, axis, step):
    pairs = [(i, i ^ step) for i in range(lax.axis_size(axis))]
    return lax.ppermute(array, axis, pairs)


def halve(part, side):
    axis, step, dim = side
    bit = lax.rem(lax.axis_index(axis) // step, 2)
    kept = lax.dynamic_slice_in_dim(part, bit, 1, dim)
    sent = lax.dynamic_slice_in_dim(part, 1 - bit, 1, dim)
    return (kept.astype(F32) + swap(sent, axis, step).astype(F32)).astype(part.dtype)


def scatter(part, sides):
    for side in sides:
        part = halve(part, side)
    return part.reshape(part.shape[4:])


def reduce_all(conv_part, down_part, qkv_part, out_part, gain_part):
    group = lax.axis_size("gx") * lax.axis_size("gy")
    width = out_part.shape[1]
    chunked = [part.reshape(group, -1, part.shape[1]) for part in (out_part, down_part, qkv_part)]
    thirds = [chunked[2][:, :, i * width : (i + 1) * width] for i in range(3)]
    early = jnp.concatenate(chunked[:2] + thirds, axis=1)
    early = scatter(
        early.reshape((2, 2, 2, 2) + early.shape[1:]), (CORE, Y, Z_NEAR, Z_FAR)
    )
    rows = chunked[0].shape[1]
    down_rows = chunked[1].shape[1]
    out_sum = early[:rows]
    down_sum = early[rows : rows + down_rows]
    third = early[rows + down_rows :].reshape(3, rows, width)
    qkv_sum = jnp.concatenate([third[0], third[1], third[2]], axis=1)
    conv_sum = scatter(
        conv_part.reshape(2, 2, 2, 2, -1, conv_part.shape[1]), (CORE, Z_NEAR, Z_FAR, Y)
    )
    for axis, step, _ in (CORE, Y, Z_NEAR, Z_FAR):
        gain_part = gain_part + swap(gain_part, axis, step)
    size = gain_part.shape[0] // group
    me = lax.axis_index(("gx", "gy"))
    gain_sum = lax.dynamic_slice_in_dim(gain_part, me * size, size, 0)
    return conv_sum, down_sum, qkv_sum, out_sum, gain_sum


def solution(mesh):
    placed = (
        P(("batch", "gx"), "gy", None, None),
        P(),
        P(),
        P(),
        P(),
        P(),
        P(("batch", "gx"), "gy", None, None),
    )
    return jax.shard_map(
        local,
        mesh=mesh,
        in_specs=placed,
        out_specs=(
            P(("batch", "gx"), "gy", None, None),
            P(("batch", "gx", "gy"), None),
            P(("batch", "gx", "gy"), None),
            P(("batch", "gx", "gy")),
            P(("batch", "gx", "gy"), None),
            P(("batch", "gx", "gy"), None),
        ),
        check_vma=False,
    )
```
